32 devices in a mesh: chain: 2 (over x), pix: 16 (over z, y, core).
Axes of the slice: x: 2, y: 2, z: 4, core: 2. Of those that a mesh axis runs over, the one named last changes fastest.
Arguments:
- latent: float32 [131072, 512], P(('chain', 'pix')), parts along dimension 0, may hold values from -6 to 6
- momentum: float32 [131072, 512], P(('chain', 'pix')), parts along dimension 0, may hold values from -6 to 6
- data: bfloat16 [512, 131072], P('pix', 'chain'), parts along dimension 1, may hold values from -6 to 6
- neighbours: int32 [8, 8], P('chain'), parts along dimension 0, may hold values from -1 to 3, as said below
- spectral_root: bfloat16 [512, 512], replicated, may hold values from -0.125 to 0.125
- log_level: float32 [512], replicated, may hold values from -0.5 to 0.5
- beam_taps: float32 [512, 65, 65], P('pix'), may hold values from -0.09375 to 0.09375
- beam_radius: int32 [512], P('pix'), may hold values from 16 to 32
- noise_weight: float32 [512], P('pix'), may hold values from 0.7 to 12.6
Outputs:
- new_latent: float32 [131072, 512], P(('chain', 'pix')), parts along dimension 0
- new_momentum: float32 [131072, 512], P(('chain', 'pix')), parts along dimension 0
- residual_maps: bfloat16 [512, 131072], P('pix', 'chain'), parts along dimension 1
- misfit: float32 [2], P('chain'), parts along dimension 0
The draws below stay inside these ranges and needn't reach their ends.
There are 2 independent parts, one for each index of `chain`. The reference program is written for one: setup_inputs(seed, part) draws one part's arguments, and reference() takes and returns one part's arrays. A program takes and returns all parts, laid end to end along the dimension named above; an argument that names none is the same for every part. Nothing has to cross between parts.
Inputs may be any that keep to these rules, and one draw needn't show every extreme that they name: The patches tile a 2 x 2 square, each cell holding one patch; neighbours[p, k] is the patch in the cell one step from p's cell in direction k, -1 where that cell lies outside the square.
All inputs are finite; a program needn't handle non-finite values.
Results may differ from the reference program's by a relative error of at most 0.0083.
Values may be sent and summed in bfloat16 or wider, within the bound.
No kernel may reach another device: no remote copies, remote signals or barrier semaphores. Data moves between devices by JAX's collectives and lax.ppermute only.
A program may use at most 192 MiB of HBM per device.

```python
import math
import jax
import jax.numpy as jnp
from jax import lax

F = 512
S = 128
R = 32
GRID = 2
PATCHES = 4
PIXELS = 65536
SPAN = 192
HALF = 97
TAPS = 65


neighbour_steps = ((-1, -1), (-1, 0), (-1, 1), (0, -1), (0, 1), (1, -1), (1, 0), (1, 1))


def draw_neighbours(key, part):
    cells = jax.random.permutation(key, PATCHES).astype(jnp.int32)
    occupant = jnp.argsort(cells).astype(jnp.int32)
    row_pos = cells // GRID
    col_pos = cells % GRID
    columns = []
    for row_step, col_step in neighbour_steps:
        next_row = row_pos + row_step
        next_col = col_pos + col_step
        valid = (next_row >= 0) & (next_row < GRID) & (next_col >= 0) & (next_col < GRID)
        target = jnp.clip(next_row * GRID + next_col, 0, PATCHES - 1)
        columns.append(jnp.where(valid, occupant[target], -1))
    return jnp.stack(columns, axis=1).astype(jnp.int32)


def draw_noise_weight(key, part):
    position = jnp.arange(F, dtype=jnp.float32) / float(F - 1)
    base_level = jnp.exp(jax.random.uniform(key, (F,), jnp.float32, math.log(0.7), math.log(1.4)))
    ramp = jnp.exp(math.log(3.0) * position)
    return (ramp * base_level).astype(jnp.float32)


def touch_ends(drawn, rng, least, top_value):
    longest = drawn.shape.index(max(drawn.shape))
    spots = []
    for shift in (0, 1):
        where = [jax.random.randint(jax.random.fold_in(rng, axis), (), 0, length) for axis, length in enumerate(drawn.shape)]
        where[longest] = (where[longest] + shift) % drawn.shape[longest]
        spots.append(tuple(where))
    return drawn.at[spots[0]].set(least).at[spots[1]].set(top_value)


def block_levels(key, shape, split, low, top_value):
    loudness, own = 1.0, jax.random.fold_in(key, 6)
    for dim, parts in split:
        draws = jnp.exp(jax.random.uniform(jax.random.fold_in(own, dim), (parts,), jnp.float32, low / len(split), top_value / len(split)))
        loudness = loudness * jnp.repeat(draws, shape[dim] // parts).reshape([-1 if axis == dim else 1 for axis in range(len(shape))])
    return loudness


def bell_draw(key, shape, scale, most, cuts=(), kind=jnp.bfloat16):
    result = scale * jax.random.normal(key, shape, jnp.float32)
    if cuts:
        result = result * block_levels(key, shape, cuts, -0.22, 0.18)
    return jnp.clip(result, -most, most).astype(kind)


def setup_inputs(seed: int = 0, part: int = 0) -> dict:
    streams_of = jax.random.split(jax.random.key(seed), 10)
    own_keys = jax.random.split(jax.random.fold_in(streams_of[9], part), 10)
    return {
        "latent": bell_draw(own_keys[0], (PIXELS, F), 1.0, 6.0, ((0, 16),), jnp.float32),
        "momentum": bell_draw(own_keys[1], (PIXELS, F), 1.0, 6.0, ((0, 16),), jnp.float32),
        "data": bell_draw(own_keys[2], (F, PIXELS), 1.0, 6.0, ((0, 16),)),
        "neighbours": draw_neighbours(jax.random.fold_in(jax.random.fold_in(streams_of[9], part), 71), part),
        "spectral_root": bell_draw(streams_of[4], (F, F), (4 * F) ** -0.5, 0.125),
        "log_level": jnp.clip(jax.random.uniform(streams_of[5], (F,), jnp.float32, -0.5, 0.5), -0.5, 0.5),
        "beam_taps": bell_draw(streams_of[6], (F, TAPS, TAPS), ((2 * R + 1) * (2 * R + 1)) ** -0.5, 0.09375, ((0, 16),), jnp.float32),
        "beam_radius": touch_ends(jax.random.randint(streams_of[7], (F,), R // 2, R + 1), jax.random.fold_in(streams_of[7], 1), R // 2, R).astype(jnp.int32),
        "noise_weight": draw_noise_weight(jax.random.fold_in(streams_of[9], 71), part),
    }


leap_size = 0.25
neighbour_steps = ((-1, -1), (-1, 0), (-1, 1), (0, -1), (0, 1), (1, -1), (1, 0), (1, 1))


def mix(form, left, right):
    return jnp.einsum(form, left.astype(jnp.float32), right.astype(jnp.float32), precision=lax.Precision.HIGHEST)


def block_range(step_value, length, reach):
    if step_value < 0:
        return length - reach, length
    if step_value > 0:
        return 0, reach
    return 0, length


def padded_range(step_value):
    if step_value < 0:
        return 0, R
    if step_value > 0:
        return R + S, SPAN
    return R, R + S


def trig_table(count_rows, count_cols):
    row_index = jnp.arange(count_rows, dtype=jnp.int32)[:, None]
    col_index = jnp.arange(count_cols, dtype=jnp.int32)[None, :]
    angle = (2.0 * math.pi / SPAN) * ((row_index * col_index) % SPAN).astype(jnp.float32)
    return jnp.cos(angle).astype(jnp.bfloat16), jnp.sin(angle).astype(jnp.bfloat16)


def inverse_weights(count_rows):
    row_index = jnp.arange(count_rows, dtype=jnp.int32)[:, None]
    freq_index = jnp.arange(HALF, dtype=jnp.int32)[None, :]
    angle = (2.0 * math.pi / SPAN) * ((row_index * freq_index) % SPAN).astype(jnp.float32)
    edge = (freq_index == 0) | (freq_index == SPAN // 2)
    factor = jnp.where(edge, jnp.float32(1.0), jnp.float32(2.0)) / float(SPAN * SPAN)
    return (factor * jnp.cos(angle)).astype(jnp.bfloat16), (factor * jnp.sin(angle)).astype(jnp.bfloat16)


def beam_spectrum(beam_taps, beam_radius):
    offsets = jnp.arange(TAPS, dtype=jnp.int32) - R
    distance = offsets[:, None] * offsets[:, None] + offsets[None, :] * offsets[None, :]
    inside = distance[None, :, :] <= (beam_radius * beam_radius)[:, None, None]
    kernel = jnp.where(inside, beam_taps, jnp.zeros_like(beam_taps))
    freq_rows = jnp.arange(HALF, dtype=jnp.int32)[:, None]
    tap_cols = jnp.arange(TAPS, dtype=jnp.int32)[None, :]
    angle_first = (2.0 * math.pi / SPAN) * ((freq_rows * tap_cols) % SPAN).astype(jnp.float32)
    tap_rows = jnp.arange(TAPS, dtype=jnp.int32)[:, None]
    freq_cols = jnp.arange(SPAN, dtype=jnp.int32)[None, :]
    angle_second = (2.0 * math.pi / SPAN) * ((tap_rows * freq_cols) % SPAN).astype(jnp.float32)
    first_cos = mix('ka,cab->ckb', jnp.cos(angle_first), kernel)
    first_sin = mix('ka,cab->ckb', jnp.sin(angle_first), kernel)
    cos_second = jnp.cos(angle_second)
    sin_second = jnp.sin(angle_second)
    spec_re = mix('ckb,bl->ckl', first_cos, cos_second) - mix('ckb,bl->ckl', first_sin, sin_second)
    spec_im = -(mix('ckb,bl->ckl', first_cos, sin_second) + mix('ckb,bl->ckl', first_sin, cos_second))
    return spec_re[:, None], spec_im[:, None]


def forward_spectrum(values):
    extent = values.shape[-1]
    cos_rows, sin_rows = trig_table(HALF, extent)
    first_cos = mix('ky,cpyx->cpkx', cos_rows, values).astype(jnp.bfloat16)
    first_sin = mix('ky,cpyx->cpkx', sin_rows, values).astype(jnp.bfloat16)
    cos_cols, sin_cols = trig_table(extent, SPAN)
    part_re = mix('cpkx,xl->cpkl', first_cos, cos_cols) - mix('cpkx,xl->cpkl', first_sin, sin_cols)
    part_im = -(mix('cpkx,xl->cpkl', first_cos, sin_cols) + mix('cpkx,xl->cpkl', first_sin, cos_cols))
    return part_re, part_im


def back_transform(prod_re, prod_im, extent):
    cos_cols, sin_cols = trig_table(SPAN, extent)
    second_re = (mix('cpkl,lx->cpkx', prod_re, cos_cols) - mix('cpkl,lx->cpkx', prod_im, sin_cols)).astype(jnp.bfloat16)
    second_im = (mix('cpkl,lx->cpkx', prod_re, sin_cols) + mix('cpkl,lx->cpkx', prod_im, cos_cols)).astype(jnp.bfloat16)
    weight_cos, weight_sin = inverse_weights(extent)
    return mix('yk,cpkx->cpyx', weight_cos, second_re) - mix('yk,cpkx->cpyx', weight_sin, second_im)


def assemble(sky_maps, neighbours):
    patch_ids = jnp.arange(PATCHES, dtype=jnp.int32)
    row_blocks = []
    for row_step in (-1, 0, 1):
        pieces = []
        for col_step in (-1, 0, 1):
            row_first, row_last = block_range(row_step, S, R)
            col_first, col_last = block_range(col_step, S, R)
            source_block = sky_maps[:, :, row_first:row_last, col_first:col_last]
            if row_step == 0 and col_step == 0:
                pieces.append(source_block)
            else:
                direction = neighbour_steps.index((row_step, col_step))
                select = (neighbours[:, direction][:, None] == patch_ids[None, :]).astype(jnp.float32)
                pieces.append(mix('pq,cqyx->cpyx', select, source_block).astype(jnp.bfloat16))
        row_blocks.append(jnp.concatenate(pieces, axis=3))
    return jnp.concatenate(row_blocks, axis=2)


def fold_back(grad_padded, neighbours):
    patch_ids = jnp.arange(PATCHES, dtype=jnp.int32)
    grad_total = grad_padded[:, :, R:R + S, R:R + S]
    for direction in range(8):
        row_step, col_step = neighbour_steps[direction]
        pad_row_first, pad_row_last = padded_range(row_step)
        pad_col_first, pad_col_last = padded_range(col_step)
        row_first, row_last = block_range(row_step, S, R)
        col_first, col_last = block_range(col_step, S, R)
        source_block = grad_padded[:, :, pad_row_first:pad_row_last, pad_col_first:pad_col_last]
        select = (neighbours[:, direction][:, None] == patch_ids[None, :]).astype(jnp.float32)
        carried = mix('pq,cpyx->cqyx', select, source_block)
        grad_total = grad_total + jnp.pad(carried, ((0, 0), (0, 0), (row_first, S - row_last), (col_first, S - col_last)))
    return grad_total


def channel_block(inputs, neighbours):
    sky_block, data_block, taps_block, radius_block, noise_block = inputs
    spec_re, spec_im = beam_spectrum(taps_block, radius_block)
    padded = assemble(sky_block, neighbours)
    part_re, part_im = forward_spectrum(padded)
    prod_re = (part_re * spec_re + part_im * spec_im).astype(jnp.bfloat16)
    prod_im = (part_im * spec_re - part_re * spec_im).astype(jnp.bfloat16)
    model_map = back_transform(prod_re, prod_im, S)
    residual = model_map - data_block.astype(jnp.float32)
    weight = noise_block[:, None, None, None]
    partial_sum = 0.5 * jnp.sum(weight * residual * residual)
    weighted = (weight * residual).astype(jnp.bfloat16)
    grad_re, grad_im = forward_spectrum(weighted)
    back_re = (grad_re * spec_re - grad_im * spec_im).astype(jnp.bfloat16)
    back_im = (grad_re * spec_im + grad_im * spec_re).astype(jnp.bfloat16)
    grad_padded = back_transform(back_re, back_im, SPAN)
    grad_sky = fold_back(grad_padded, neighbours)
    grad_log = (grad_sky * sky_block.astype(jnp.float32)).astype(jnp.bfloat16)
    return residual.astype(jnp.bfloat16), partial_sum, grad_log


def reference(latent, momentum, data, neighbours, spectral_root, log_level, beam_taps, beam_radius, noise_weight):
    latent_low = latent.astype(jnp.bfloat16)
    log_sky = jnp.dot(latent_low, spectral_root.T, preferred_element_type=jnp.float32) + log_level[None, :]
    sky_rows = jnp.exp(log_sky).astype(jnp.bfloat16)
    sky_maps = sky_rows.T.reshape(F, PATCHES, S, S)
    data_maps = data.reshape(F, PATCHES, S, S)
    blocks = F // 8
    inputs = (sky_maps.reshape(blocks, 8, PATCHES, S, S), data_maps.reshape(blocks, 8, PATCHES, S, S),
              beam_taps.reshape(blocks, 8, TAPS, TAPS), beam_radius.reshape(blocks, 8),
              noise_weight.reshape(blocks, 8))
    residual, partials, grad_log = lax.map(partial_block(neighbours), inputs)
    misfit = (jnp.sum(partials) / (F * PIXELS)).reshape(1)
    grad_rows = grad_log.reshape(F, PIXELS)
    grad_latent = jnp.dot(grad_rows.T, spectral_root, preferred_element_type=jnp.float32)
    new_momentum = momentum - leap_size * (latent + grad_latent)
    new_latent = latent + leap_size * new_momentum
    return new_latent, new_momentum, residual.reshape(F, PIXELS), misfit


def partial_block(neighbours):
    def apply_block(inputs):
        return channel_block(inputs, neighbours)
    return apply_block
```

```python
import functools
import math

import jax
import jax.numpy as jnp
import numpy as np
from jax import lax
from jax.experimental import pallas as pl
from jax.experimental.pallas import tpu as pltpu
from jax.sharding import PartitionSpec as P

S = 128
R = 32
PATCHES = 4
TAPS = 65
SIDE = 2 * S
SPAN = SIDE + R
HALF = SPAN // 2
LANES = 256
TAP_ROWS = 80
TAP_LANES = 128
BLOCK = 16

leap_size = 0.25


def half_tables(positions):
    angle = 2.0 * math.pi / SPAN * (np.arange(HALF)[:, None] + 0.5) * positions[None, :]
    return np.cos(angle), np.sin(angle)


def tables():
    low = jnp.bfloat16
    cos_image, sin_image = half_tables(np.arange(SIDE))
    cos_taps, sin_taps = half_tables(np.arange(TAPS) - R)
    rows = np.concatenate([cos_image, sin_image], axis=0)
    cols = np.zeros((2 * LANES, SIDE))
    cols[:HALF] = cos_image
    cols[LANES : LANES + HALF] = sin_image
    tap_rows = np.zeros((SPAN, TAP_ROWS))
    tap_rows[:, :TAPS] = np.concatenate([cos_taps, sin_taps], axis=0)
    tap_cols = np.zeros((TAP_LANES, 2 * LANES))
    tap_cols[:TAPS, :HALF] = cos_taps.T
    tap_cols[:TAPS, LANES : LANES + HALF] = sin_taps.T
    return (
        np.asarray(rows, low),
        np.asarray(rows.T, low),
        np.asarray(cols, low),
        np.asarray(cols.T, low),
        np.asarray(np.concatenate([tap_rows, tap_rows], axis=1), low),
        np.asarray(np.concatenate([tap_cols, tap_cols], axis=0), low),
    )


def dot(left, right):
    return lax.dot_general(
        left, right, (((1,), (0,)), ((), ())), preferred_element_type=jnp.float32
    )


def split_low(values):
    high = values.astype(jnp.bfloat16)
    return high, (values - high.astype(jnp.float32)).astype(jnp.bfloat16)


def convolve_kernel(
    strip_rows,
    order_ref,
    noise_ref,
    sky_ref,
    data_ref,
    taps_ref,
    rows_ref,
    rows_t_ref,
    cols_ref,
    cols_t_ref,
    tap_rows_ref,
    tap_cols_ref,
    residual_ref,
    grad_ref,
    misfit_ref,
    image_ref,
    data_image_ref,
):
    strips = S // strip_rows
    channels = sky_ref.shape[1]

    def strip_loop(body):
        def step(index, carry):
            cell = index // strips
            strip = index % strips
            cell_row, cell_col = cell // 2, cell % 2
            patch = order_ref[cell]
            device = patch * strips + strip
            base = cell_row * S + strip * strip_rows
            pixel_base = device * (strip_rows * S)
            for row in range(strip_rows):
                body(
                    cell_col,
                    device,
                    row,
                    pl.ds(base + row, channels, stride=SIDE),
                    pl.ds(pl.multiple_of(pixel_base + row * S, S), S),
                )
            return carry

        lax.fori_loop(0, PATCHES * strips, step, 0)

    def spread(cell_col, device, row, spread_rows, pixels):
        lanes = pl.ds(row * S, S)
        image_ref[cell_col, spread_rows, :] = sky_ref[device, :, lanes].astype(jnp.float32)
        data_image_ref[cell_col, spread_rows, :] = data_ref[:, pixels].astype(jnp.float32)

    def gather(cell_col, device, row, spread_rows, pixels):
        lanes = pl.ds(row * S, S)
        grad_ref[device, :, lanes] = image_ref[cell_col, spread_rows, :].astype(jnp.bfloat16)
        residual_ref[:, pixels] = data_image_ref[cell_col, spread_rows, :].astype(jnp.bfloat16)

    def quarters(values):
        return (
            values[:HALF, :LANES],
            values[:HALF, LANES:],
            values[HALF:, :LANES],
            values[HALF:, LANES:],
        )

    def signed_pair(values):
        cc, cs, sc, ss = quarters(values)
        return cc - ss, sc + cs, cc + ss, sc - cs

    def filter_image(image, beam, conjugate):
        first = dot(rows_ref[...], image).astype(jnp.bfloat16)
        re_plus, im_plus, re_minus, im_minus = signed_pair(dot(first, cols_t_ref[...]))
        beam_re_plus, beam_im_plus, beam_re_minus, beam_im_minus = beam
        if conjugate:
            out_re_plus = re_plus * beam_re_plus + im_plus * beam_im_plus
            out_im_plus = im_plus * beam_re_plus - re_plus * beam_im_plus
            out_re_minus = re_minus * beam_re_minus + im_minus * beam_im_minus
            out_im_minus = im_minus * beam_re_minus - re_minus * beam_im_minus
        else:
            out_re_plus = re_plus * beam_re_plus - im_plus * beam_im_plus
            out_im_plus = im_plus * beam_re_plus + re_plus * beam_im_plus
            out_re_minus = re_minus * beam_re_minus - im_minus * beam_im_minus
            out_im_minus = im_minus * beam_re_minus + re_minus * beam_im_minus
        product = jnp.concatenate(
            [
                jnp.concatenate([out_re_plus + out_re_minus, out_im_plus - out_im_minus], axis=1),
                jnp.concatenate([out_im_plus + out_im_minus, out_re_minus - out_re_plus], axis=1),
            ],
            axis=0,
        ).astype(jnp.bfloat16)
        second = dot(product, cols_ref[...]).astype(jnp.bfloat16)
        return dot(rows_t_ref[...], second)

    def channel_step(channel, carry):
        here = pl.ds(pl.multiple_of(channel * SIDE, SIDE), SIDE)
        tap_high, tap_low = split_low(taps_ref[channel])
        tap_first = dot(tap_rows_ref[...], jnp.concatenate([tap_high, tap_low], axis=0))
        first_high, first_low = split_low(tap_first * (2.0 / (SPAN * SPAN)))
        spectrum = dot(jnp.concatenate([first_high, first_low], axis=1), tap_cols_ref[...])
        beam = signed_pair(spectrum)
        image = jnp.concatenate([image_ref[0, here, :], image_ref[1, here, :]], axis=1)
        model = filter_image(image.astype(jnp.bfloat16), beam, True)
        data = jnp.concatenate([data_image_ref[0, here, :], data_image_ref[1, here, :]], axis=1)
        residual = model - data
        data_image_ref[0, here, :] = residual[:, :S]
        data_image_ref[1, here, :] = residual[:, S:]
        weighted = noise_ref[channel] * residual
        misfit_ref[...] += jnp.sum((weighted * residual).reshape(SIDE // 8, 8, SIDE), axis=0)
        grad = filter_image(weighted.astype(jnp.bfloat16), beam, False) * image
        image_ref[0, here, :] = grad[:, :S]
        image_ref[1, here, :] = grad[:, S:]
        return carry

    misfit_ref[...] = jnp.zeros_like(misfit_ref)
    strip_loop(spread)
    lax.fori_loop(0, channels, channel_step, 0)
    strip_loop(gather)


def convolve(order, noise_weight, sky, data, taps):
    devices, channels, strip = sky.shape
    smem = pl.BlockSpec(memory_space=pltpu.SMEM)
    vmem = pl.BlockSpec(memory_space=pltpu.VMEM)
    constants = tables()
    pixels = devices * strip
    macs = channels * (2 * 1952 + 1440) * 256 * 256
    return pl.pallas_call(
        functools.partial(convolve_kernel, strip // S),
        out_shape=(
            jax.ShapeDtypeStruct((channels, pixels), jnp.bfloat16),
            jax.ShapeDtypeStruct(sky.shape, jnp.bfloat16),
            jax.ShapeDtypeStruct((8, SIDE), jnp.float32),
        ),
        in_specs=[smem, smem] + [vmem] * (3 + len(constants)),
        out_specs=(vmem, vmem, vmem),
        scratch_shapes=[
            pltpu.VMEM((2, channels * SIDE, S), jnp.float32),
            pltpu.VMEM((2, channels * SIDE, S), jnp.float32),
        ],
        compiler_params=pltpu.CompilerParams(vmem_limit_bytes=44 * 1024 * 1024),
        cost_estimate=pl.CostEstimate(
            flops=2 * macs, bytes_accessed=8 * channels * pixels, transcendentals=0
        ),
    )(order, noise_weight, sky, data, taps, *constants)


def cell_order(neighbours):
    has_above = neighbours[:, 1] != -1
    has_left = neighbours[:, 3] != -1
    cells = 2 * has_above.astype(jnp.int32) + has_left.astype(jnp.int32)
    patch_ids = jnp.arange(PATCHES, dtype=jnp.int32)
    match = cells[None, :] == patch_ids[:, None]
    return jnp.sum(jnp.where(match, patch_ids[None, :], 0), axis=1)


def masked_taps(beam_taps, beam_radius):
    offsets = jnp.arange(TAPS, dtype=jnp.int32) - R
    distance = offsets[:, None] * offsets[:, None] + offsets[None, :] * offsets[None, :]
    inside = distance[None, :, :] <= (beam_radius * beam_radius)[:, None, None]
    kernel = jnp.where(inside, beam_taps, jnp.zeros_like(beam_taps))
    return jnp.pad(kernel, ((0, 0), (0, TAP_ROWS - TAPS), (0, TAP_LANES - TAPS)))


def shards(
    latent,
    momentum,
    data,
    neighbours,
    spectral_root,
    log_level,
    beam_taps,
    beam_radius,
    noise_weight,
):
    devices = lax.axis_size("pix")
    pix_dev = latent.shape[0]
    chan_dev = data.shape[0]
    freqs = spectral_root.shape[0]
    chunks = chan_dev // BLOCK
    latent_low = latent.astype(jnp.bfloat16)
    root_parts = spectral_root.reshape(devices, chunks, BLOCK, freqs)
    level_parts = log_level.reshape(devices, chunks, BLOCK)
    order = cell_order(neighbours)
    taps = masked_taps(beam_taps, beam_radius)

    skies = []
    for chunk in range(chunks):
        root = root_parts[:, chunk].reshape(devices * BLOCK, freqs)
        level = level_parts[:, chunk].reshape(devices * BLOCK)
        log_sky = lax.dot_general(
            root, latent_low, (((1,), (1,)), ((), ())), preferred_element_type=jnp.float32
        )
        sky = jnp.exp(log_sky + level[:, None]).astype(jnp.bfloat16)
        skies.append(sky.reshape(devices, BLOCK, pix_dev))

    residuals, partials, grads = [], [], []
    for chunk in range(chunks):
        here = slice(chunk * BLOCK, (chunk + 1) * BLOCK)
        sky = lax.all_to_all(skies[chunk], "pix", split_axis=0, concat_axis=0, tiled=True)
        residual, grad, partial = convolve(order, noise_weight[here], sky, data[here], taps[here])
        residuals.append(residual)
        partials.append(jnp.sum(partial))
        grads.append(lax.all_to_all(grad, "pix", split_axis=0, concat_axis=0, tiled=True))

    misfit = (0.5 * lax.psum(sum(partials), "pix") / (freqs * devices * pix_dev)).reshape(1)
    grad_latent = 0.0
    for chunk in range(chunks):
        grad_latent = grad_latent + lax.dot_general(
            grads[chunk].reshape(devices * BLOCK, pix_dev),
            root_parts[:, chunk].reshape(devices * BLOCK, freqs),
            (((0,), (0,)), ((), ())),
            preferred_element_type=jnp.float32,
        )
    new_momentum = momentum - leap_size * (latent + grad_latent)
    new_latent = latent + leap_size * new_momentum
    residual_maps = jnp.concatenate(residuals, axis=0)
    return (new_latent, new_momentum, residual_maps, misfit)


def solution(mesh):
    placed = (
        P(("chain", "pix"), None),
        P(("chain", "pix"), None),
        P("pix", "chain"),
        P("chain", None),
        P(),
        P(),
        P("pix", None, None),
        P("pix"),
        P("pix"),
    )
    return jax.shard_map(
        shards,
        mesh=mesh,
        in_specs=placed,
        out_specs=(
            P(("chain", "pix"), None),
            P(("chain", "pix"), None),
            P("pix", "chain"),
            P("chain"),
        ),
        check_vma=False,
    )
```

```python
import functools
import math

import jax
import jax.numpy as jnp
import numpy as np
from jax import lax
from jax.experimental import pallas as pl
from jax.experimental.pallas import tpu as pltpu
from jax.sharding import PartitionSpec as P

S = 128
R = 32
PATCHES = 4
TAPS = 65
SIDE = 2 * S
SPAN = SIDE + R
HALF = SPAN // 2
LANES = 256
TAP_ROWS = 80
TAP_LANES = 128
BLOCK = 16
VMEM_BYTES = 56 * 1024 * 1024
FLATTEN_VMEM_BYTES = 24 * 1024 * 1024
PIXEL_BLOCK = 1024
SKY_BLOCK = 2048

leap_size = 0.25


def half_tables(positions):
    angle = 2.0 * math.pi / SPAN * (np.arange(HALF)[:, None] + 0.5) * positions[None, :]
    return np.cos(angle), np.sin(angle)


def tables():
    low = jnp.bfloat16
    cos_image, sin_image = half_tables(np.arange(SIDE))
    cos_taps, sin_taps = half_tables(np.arange(TAPS) - R)
    rows = np.concatenate([cos_image, sin_image], axis=0)
    cols = np.zeros((2 * LANES, SIDE))
    cols[:HALF] = cos_image
    cols[LANES : LANES + HALF] = sin_image
    tap_rows = np.zeros((SPAN, TAP_ROWS))
    tap_rows[:, :TAPS] = np.concatenate([cos_taps, sin_taps], axis=0)
    tap_cols = np.zeros((TAP_LANES, 2 * LANES))
    tap_cols[:TAPS, :HALF] = cos_taps.T
    tap_cols[:TAPS, LANES : LANES + HALF] = sin_taps.T
    return (
        np.asarray(rows, low),
        np.asarray(rows.T, low),
        np.asarray(cols, low),
        np.asarray(cols.T, low),
        np.asarray(np.concatenate([tap_rows, tap_rows], axis=1), low),
        np.asarray(np.concatenate([tap_cols, tap_cols], axis=0), low),
    )


def dot(left, right):
    return lax.dot_general(
        left, right, (((1,), (0,)), ((), ())), preferred_element_type=jnp.float32
    )


def split_low(values):
    high = values.astype(jnp.bfloat16)
    return high, (values - high.astype(jnp.float32)).astype(jnp.bfloat16)


def strip_loop(order_ref, strip_rows, channels, body):
    strips = S // strip_rows

    def step(index, carry):
        cell = index // strips
        strip = index % strips
        device = order_ref[cell] * strips + strip
        base = (cell // 2) * S + strip * strip_rows
        pixel_base = device * (strip_rows * S)
        for row in range(strip_rows):
            body(
                cell % 2,
                device,
                pl.ds(row * S, S),
                pl.ds(base + row, channels, stride=SIDE),
                pl.ds(pl.multiple_of(pixel_base + row * S, S), S),
            )
        return carry

    lax.fori_loop(0, PATCHES * strips, step, 0)


def channel_rows(channel):
    return pl.ds(pl.multiple_of(channel * SIDE, SIDE), SIDE)


def signed_pair(values):
    cc, cs = values[:HALF, :LANES], values[:HALF, LANES:]
    sc, ss = values[HALF:, :LANES], values[HALF:, LANES:]
    return cc - ss, sc + cs, cc + ss, sc - cs


def prepare_kernel(
    strip_rows, order_ref, data_ref, taps_ref, tap_rows_ref, tap_cols_ref, beam_ref, image_ref, stack_ref
):
    channels = data_ref.shape[0]

    def spread(cell_col, device, lanes, spread_rows, pixels):
        stack_ref[cell_col, spread_rows, :] = data_ref[:, pixels].astype(jnp.float32)

    def channel_step(channel, carry):
        tap_high, tap_low = split_low(taps_ref[channel])
        tap_first = dot(tap_rows_ref[...], jnp.concatenate([tap_high, tap_low], axis=0))
        first_high, first_low = split_low(tap_first * (2.0 / (SPAN * SPAN)))
        spectrum = dot(jnp.concatenate([first_high, first_low], axis=1), tap_cols_ref[...])
        for part, values in enumerate(signed_pair(spectrum)):
            beam_ref[channel, part] = values
        here = channel_rows(channel)
        image_ref[channel, :, :S] = stack_ref[0, here, :].astype(jnp.bfloat16)
        image_ref[channel, :, S:] = stack_ref[1, here, :].astype(jnp.bfloat16)
        return carry

    strip_loop(order_ref, strip_rows, channels, spread)
    lax.fori_loop(0, channels, channel_step, 0)


def prepare(order, data, taps, strip_rows):
    channels, pixels = data.shape
    constants = tables()[4:]
    whole = pl.BlockSpec(memory_space=pltpu.VMEM)
    return pl.pallas_call(
        functools.partial(prepare_kernel, strip_rows),
        out_shape=(
            jax.ShapeDtypeStruct((channels, 4, HALF, LANES), jnp.float32),
            jax.ShapeDtypeStruct((channels, SIDE, SIDE), jnp.bfloat16),
        ),
        grid=(channels // BLOCK,),
        in_specs=[
            pl.BlockSpec(memory_space=pltpu.SMEM),
            pl.BlockSpec((BLOCK, pixels), lambda i: (i, 0)),
            pl.BlockSpec((BLOCK, TAP_ROWS, TAP_LANES), lambda i: (i, 0, 0)),
            whole,
            whole,
        ],
        out_specs=(
            pl.BlockSpec((BLOCK, 4, HALF, LANES), lambda i: (i, 0, 0, 0)),
            pl.BlockSpec((BLOCK, SIDE, SIDE), lambda i: (i, 0, 0)),
        ),
        scratch_shapes=[pltpu.VMEM((2, BLOCK * SIDE, S), jnp.float32)],
        compiler_params=pltpu.CompilerParams(vmem_limit_bytes=VMEM_BYTES),
        cost_estimate=pl.CostEstimate(
            flops=2 * channels * 1440 * 65536, bytes_accessed=28 << 20, transcendentals=0
        ),
    )(order, data, taps, *constants)


def convolve_kernel(
    strip_rows,
    first_channel,
    order_ref,
    noise_ref,
    earlier_ref,
    sky_ref,
    beam_ref,
    data_ref,
    rows_ref,
    rows_t_ref,
    cols_ref,
    cols_t_ref,
    residual_ref,
    grad_ref,
    misfit_ref,
    stack_ref,
):
    channel = pl.program_id(0)
    channels = sky_ref.shape[1]

    def spread(cell_col, device, lanes, spread_rows, pixels):
        stack_ref[cell_col, spread_rows, :] = sky_ref[device, :, lanes].astype(jnp.float32)

    def gather(cell_col, device, lanes, spread_rows, pixels):
        grad_ref[device, :, lanes] = stack_ref[cell_col, spread_rows, :].astype(jnp.bfloat16)

    def filter_image(image, conjugate):
        first = dot(rows_ref[...], image).astype(jnp.bfloat16)
        re_plus, im_plus, re_minus, im_minus = signed_pair(dot(first, cols_t_ref[...]))
        beam_re_plus, beam_im_plus, beam_re_minus, beam_im_minus = (
            beam_ref[0, 0],
            beam_ref[0, 1],
            beam_ref[0, 2],
            beam_ref[0, 3],
        )
        if conjugate:
            out_re_plus = re_plus * beam_re_plus + im_plus * beam_im_plus
            out_im_plus = im_plus * beam_re_plus - re_plus * beam_im_plus
            out_re_minus = re_minus * beam_re_minus + im_minus * beam_im_minus
            out_im_minus = im_minus * beam_re_minus - re_minus * beam_im_minus
        else:
            out_re_plus = re_plus * beam_re_plus - im_plus * beam_im_plus
            out_im_plus = im_plus * beam_re_plus + re_plus * beam_im_plus
            out_re_minus = re_minus * beam_re_minus - im_minus * beam_im_minus
            out_im_minus = im_minus * beam_re_minus + re_minus * beam_im_minus
        product = jnp.concatenate(
            [
                jnp.concatenate([out_re_plus + out_re_minus, out_im_plus - out_im_minus], axis=1),
                jnp.concatenate([out_im_plus + out_im_minus, out_re_minus - out_re_plus], axis=1),
            ],
            axis=0,
        ).astype(jnp.bfloat16)
        second = dot(product, cols_ref[...]).astype(jnp.bfloat16)
        return dot(rows_t_ref[...], second)

    @pl.when(channel == 0)
    def _():
        misfit_ref[...] = earlier_ref[...]
        strip_loop(order_ref, strip_rows, channels, spread)

    here = channel_rows(channel)
    image = jnp.concatenate([stack_ref[0, here, :], stack_ref[1, here, :]], axis=1)
    residual = filter_image(image.astype(jnp.bfloat16), True) - data_ref[0].astype(jnp.float32)
    residual_ref[0] = residual.astype(jnp.bfloat16)
    weighted = noise_ref[first_channel + channel] * residual
    misfit_ref[...] += jnp.sum((weighted * residual).reshape(SIDE // 8, 8, SIDE), axis=0)
    grad = filter_image(weighted.astype(jnp.bfloat16), False) * image
    stack_ref[0, here, :] = grad[:, :S]
    stack_ref[1, here, :] = grad[:, S:]

    @pl.when(channel == channels - 1)
    def _():
        strip_loop(order_ref, strip_rows, channels, gather)
        strip = strip_rows * S
        if grad_ref.shape[2] > strip:
            total = jnp.full((channels, S), jnp.sum(misfit_ref[...]), jnp.float32)
            high, rest = split_low(total)
            middle = rest.astype(jnp.float32)
            low = total - high.astype(jnp.float32) - middle
            lane = lax.broadcasted_iota(jnp.int32, (channels, S), 1)
            terms = jnp.where(lane == 0, high.astype(jnp.float32), jnp.where(lane == 1, middle, low))
            terms = jnp.where(lane < 3, terms, 0.0).astype(jnp.bfloat16)
            for device in range(grad_ref.shape[0]):
                grad_ref[device, :, strip:] = terms


def convolve(order, noise_weight, earlier, sky, beam, data_images, chunk, extra):
    devices, channels, strip = sky.shape
    smem = pl.BlockSpec(memory_space=pltpu.SMEM)
    whole = pl.BlockSpec(memory_space=pltpu.VMEM)
    constants = tables()[:4]
    first_channel = chunk * channels
    return pl.pallas_call(
        functools.partial(convolve_kernel, strip // S, first_channel),
        out_shape=(
            jax.ShapeDtypeStruct((channels, SIDE, SIDE), jnp.bfloat16),
            jax.ShapeDtypeStruct((devices, channels, strip + extra), jnp.bfloat16),
            jax.ShapeDtypeStruct((8, SIDE), jnp.float32),
        ),
        grid=(channels,),
        in_specs=[
            smem,
            smem,
            whole,
            whole,
            pl.BlockSpec((1, 4, HALF, LANES), lambda i: (first_channel + i, 0, 0, 0)),
            pl.BlockSpec((1, SIDE, SIDE), lambda i: (first_channel + i, 0, 0)),
        ]
        + [whole] * len(constants),
        out_specs=(pl.BlockSpec((1, SIDE, SIDE), lambda i: (i, 0, 0)), whole, whole),
        scratch_shapes=[pltpu.VMEM((2, channels * SIDE, S), jnp.float32)],
        compiler_params=pltpu.CompilerParams(vmem_limit_bytes=VMEM_BYTES),
        cost_estimate=pl.CostEstimate(
            flops=2 * channels * 2 * 1952 * 65536, bytes_accessed=24 << 20, transcendentals=0
        ),
    )(order, noise_weight, earlier, sky, beam, data_images, *constants)


def flatten_kernel(strip_rows, order_ref, *refs):
    image_refs, flat_ref, stack_ref = refs[:-2], refs[-2], refs[-1]
    for chunk, image_ref in enumerate(image_refs):
        channels = image_ref.shape[0]
        rows = slice(chunk * channels, (chunk + 1) * channels)

        def channel_step(channel, carry):
            here = channel_rows(channel)
            image = image_ref[channel].astype(jnp.float32)
            stack_ref[0, here, :] = image[:, :S]
            stack_ref[1, here, :] = image[:, S:]
            return carry

        def gather(cell_col, device, lanes, spread_rows, pixels):
            flat_ref[rows, pixels] = stack_ref[cell_col, spread_rows, :].astype(jnp.bfloat16)

        lax.fori_loop(0, channels, channel_step, 0)
        strip_loop(order_ref, strip_rows, channels, gather)


def flatten(order, images, strip_rows):
    channels = sum(part.shape[0] for part in images)
    whole = pl.BlockSpec(memory_space=pltpu.VMEM)
    return pl.pallas_call(
        functools.partial(flatten_kernel, strip_rows),
        out_shape=jax.ShapeDtypeStruct((channels, SIDE * SIDE), jnp.bfloat16),
        in_specs=[pl.BlockSpec(memory_space=pltpu.SMEM)] + [whole] * len(images),
        out_specs=whole,
        scratch_shapes=[pltpu.VMEM((2, images[0].shape[0] * SIDE, S), jnp.float32)],
        compiler_params=pltpu.CompilerParams(vmem_limit_bytes=FLATTEN_VMEM_BYTES),
        cost_estimate=pl.CostEstimate(flops=1 << 20, bytes_accessed=32 << 20, transcendentals=0),
    )(order, *images)


def sky_kernel(chunk, root_ref, level_ref, latent_ref, sky_ref):
    devices, _, channels, freqs = root_ref.shape
    pixels = latent_ref.shape[0]
    root = root_ref[:, 0].reshape(devices * channels, freqs)
    log_sky = lax.dot_general(
        root,
        latent_ref[...].astype(jnp.bfloat16),
        (((1,), (1,)), ((), ())),
        preferred_element_type=jnp.float32,
    )
    level = jnp.broadcast_to(level_ref[...], (S, freqs)).T.reshape(devices, -1, channels, S)
    level = level[:, chunk].reshape(devices * channels, S)
    for first in range(0, pixels, S):
        sky = jnp.exp(log_sky[:, first : first + S] + level).astype(jnp.bfloat16)
        sky_ref[:, :, first : first + S] = sky.reshape(devices, channels, S)


def brightness(chunk, root_parts, log_level, latent):
    devices, _, channels, freqs = root_parts.shape
    pixels = latent.shape[0]
    return pl.pallas_call(
        functools.partial(sky_kernel, chunk),
        out_shape=jax.ShapeDtypeStruct((devices, channels, pixels), jnp.bfloat16),
        grid=(pixels // SKY_BLOCK,),
        in_specs=[
            pl.BlockSpec((devices, 1, channels, freqs), lambda i: (0, chunk, 0, 0)),
            pl.BlockSpec((1, freqs), lambda i: (0, 0)),
            pl.BlockSpec((SKY_BLOCK, freqs), lambda i: (i, 0)),
        ],
        out_specs=pl.BlockSpec((devices, channels, SKY_BLOCK), lambda i: (0, 0, i)),
        compiler_params=pltpu.CompilerParams(vmem_limit_bytes=VMEM_BYTES),
        cost_estimate=pl.CostEstimate(
            flops=2 * pixels * freqs * devices * channels,
            bytes_accessed=10 << 20,
            transcendentals=pixels * devices * channels,
        ),
    )(root_parts, log_level.reshape(1, freqs), latent)


def pull_back(chunk, grad_ref, root_ref, here):
    devices, channels, _ = grad_ref.shape
    return lax.dot_general(
        grad_ref[:, :, here].reshape(devices * channels, here.size),
        root_ref[:, chunk].reshape(devices * channels, -1),
        (((0,), (0,)), ((), ())),
        preferred_element_type=jnp.float32,
    )


def kick_kernel(grad_count, momentum_ref, latent_ref, root_ref, *refs):
    far_refs, kicked_ref, grad_refs = refs[:grad_count], refs[grad_count], refs[grad_count + 1 :]
    pixels = latent_ref.shape[0]
    here = pl.ds(pl.multiple_of(pl.program_id(0) * pixels, pixels), pixels)

    @pl.when(pl.program_id(0) == 0)
    def _():
        for far_ref, grad_ref in zip(far_refs, grad_refs):
            pltpu.sync_copy(far_ref, grad_ref)

    force = latent_ref[...]
    for chunk, grad_ref in enumerate(grad_refs):
        force = force + pull_back(chunk, grad_ref, root_ref, here)
    kicked_ref[...] = momentum_ref[...] - leap_size * force


def kick(momentum, latent, root_parts, grads):
    pixels, freqs = latent.shape
    block = pl.BlockSpec((PIXEL_BLOCK, freqs), lambda i: (i, 0))
    far = pl.BlockSpec(memory_space=pltpu.HBM)
    return pl.pallas_call(
        functools.partial(kick_kernel, len(grads)),
        out_shape=jax.ShapeDtypeStruct(latent.shape, jnp.float32),
        grid=(pixels // PIXEL_BLOCK,),
        in_specs=[block, block, pl.BlockSpec(memory_space=pltpu.VMEM)] + [far] * len(grads),
        out_specs=block,
        scratch_shapes=[pltpu.VMEM(grad.shape, grad.dtype) for grad in grads],
        compiler_params=pltpu.CompilerParams(vmem_limit_bytes=VMEM_BYTES),
        cost_estimate=pl.CostEstimate(
            flops=2 * pixels * freqs * 256, bytes_accessed=26 << 20, transcendentals=0
        ),
    )(momentum, latent, root_parts, *grads)


def leap_kernel(
    chunk,
    scale,
    kicked_ref,
    latent_ref,
    grad_ref,
    root_ref,
    latent_out_ref,
    momentum_out_ref,
    misfit_ref,
):
    pixels = momentum_out_ref.shape[0]
    here = pl.ds(pl.multiple_of(pl.program_id(0) * pixels, pixels), pixels)
    grad_latent = pull_back(chunk, grad_ref, root_ref, here)
    momentum = kicked_ref[...] - leap_size * grad_latent
    momentum_out_ref[...] = momentum
    latent_out_ref[...] = latent_ref[...] + leap_size * momentum

    @pl.when(pl.program_id(0) == 0)
    def _():
        terms = grad_ref[:, :, grad_ref.shape[2] - S :].astype(jnp.float32)
        row = lax.broadcasted_iota(jnp.int32, terms.shape, 1)
        misfit_ref[0] = scale * jnp.sum(jnp.where(row == 0, terms, 0.0))


def leap(chunk, scale, kicked, latent, grad, root_parts):
    pixels, freqs = latent.shape
    whole = pl.BlockSpec(memory_space=pltpu.VMEM)
    block = pl.BlockSpec((PIXEL_BLOCK, freqs), lambda i: (i, 0))
    return pl.pallas_call(
        functools.partial(leap_kernel, chunk, scale),
        out_shape=(jax.ShapeDtypeStruct(latent.shape, jnp.float32),) * 2
        + (jax.ShapeDtypeStruct((1,), jnp.float32),),
        grid=(pixels // PIXEL_BLOCK,),
        in_specs=[block, block, whole, whole],
        out_specs=(block, block, pl.BlockSpec(memory_space=pltpu.SMEM)),
        compiler_params=pltpu.CompilerParams(vmem_limit_bytes=VMEM_BYTES),
        cost_estimate=pl.CostEstimate(
            flops=2 * pixels * freqs * 256, bytes_accessed=34 << 20, transcendentals=0
        ),
    )(kicked, latent, grad, root_parts)


def cell_order(neighbours):
    has_above = neighbours[:, 1] != -1
    has_left = neighbours[:, 3] != -1
    cells = 2 * has_above.astype(jnp.int32) + has_left.astype(jnp.int32)
    patch_ids = jnp.arange(PATCHES, dtype=jnp.int32)
    match = cells[None, :] == patch_ids[:, None]
    return jnp.sum(jnp.where(match, patch_ids[None, :], 0), axis=1)


def masked_taps(beam_taps, beam_radius):
    offsets = jnp.arange(TAPS, dtype=jnp.int32) - R
    distance = offsets[:, None] * offsets[:, None] + offsets[None, :] * offsets[None, :]
    inside = distance[None, :, :] <= (beam_radius * beam_radius)[:, None, None]
    kernel = jnp.where(inside, beam_taps, jnp.zeros_like(beam_taps))
    return jnp.pad(kernel, ((0, 0), (0, TAP_ROWS - TAPS), (0, TAP_LANES - TAPS)))


def shards(
    latent,
    momentum,
    data,
    neighbours,
    spectral_root,
    log_level,
    beam_taps,
    beam_radius,
    noise_weight,
):
    devices = lax.axis_size("pix")
    pix_dev = latent.shape[0]
    chan_dev = data.shape[0]
    freqs = spectral_root.shape[0]
    chunks = chan_dev // BLOCK
    root_parts = spectral_root.reshape(devices, chunks, BLOCK, freqs)
    order = cell_order(neighbours)
    taps = masked_taps(beam_taps, beam_radius)

    strip_rows = pix_dev // S
    beam, data_images = prepare(order, data, taps, strip_rows)

    skies = []
    for chunk in range(chunks):
        level = log_level
        if chunk == 1:
            level, beam, data_images = lax.optimization_barrier((level, beam, data_images))
        skies.append(brightness(chunk, root_parts, level, latent))

    residuals, grads = [], []
    partial = jnp.zeros((8, SIDE), jnp.float32)
    for chunk in range(chunks):
        extra = S if chunk == chunks - 1 else 0
        sky = lax.all_to_all(skies[chunk], "pix", split_axis=0, concat_axis=0, tiled=True)
        residual, grad, partial = convolve(
            order, noise_weight, partial, sky, beam, data_images, chunk, extra
        )
        residuals.append(residual)
        grads.append(lax.all_to_all(grad, "pix", split_axis=0, concat_axis=0, tiled=True))

    residual_maps = flatten(order, residuals, strip_rows)
    kicked = kick(momentum, latent, root_parts, grads[:-1])
    scale = 0.5 / (freqs * devices * pix_dev)
    new_latent, new_momentum, misfit = leap(
        chunks - 1, scale, kicked, latent, grads[-1], root_parts
    )
    return (new_latent, new_momentum, residual_maps, misfit)


def solution(mesh):
    placed = (
        P(("chain", "pix"), None),
        P(("chain", "pix"), None),
        P("pix", "chain"),
        P("chain", None),
        P(),
        P(),
        P("pix", None, None),
        P("pix"),
        P("pix"),
    )
    return jax.shard_map(
        shards,
        mesh=mesh,
        in_specs=placed,
        out_specs=(
            P(("chain", "pix"), None),
            P(("chain", "pix"), None),
            P("pix", "chain"),
            P("chain"),
        ),
        check_vma=False,
    )
```

```python
import functools
import math

import jax
import jax.numpy as jnp
import numpy as np
from jax import lax
from jax.experimental import pallas as pl
from jax.experimental.pallas import tpu as pltpu
from jax.sharding import PartitionSpec as P

S = 128
R = 32
PATCHES = 4
TAPS = 65
SIDE = 2 * S
SPAN = SIDE + R
HALF = SPAN // 2
LANES = 256
TAP_ROWS = 80
TAP_LANES = 128
BLOCK = 16
VMEM_BYTES = 56 * 1024 * 1024
FLATTEN_VMEM_BYTES = 24 * 1024 * 1024
PIXEL_BLOCK = 1024
SKY_BLOCK = 2048

leap_size = 0.25


def half_tables(positions):
    angle = 2.0 * math.pi / SPAN * (np.arange(HALF)[:, None] + 0.5) * positions[None, :]
    return np.cos(angle), np.sin(angle)


def tables():
    low = jnp.bfloat16
    cos_image, sin_image = half_tables(np.arange(SIDE))
    cos_taps, sin_taps = half_tables(np.arange(TAPS) - R)
    rows = np.concatenate([cos_image, sin_image], axis=0)
    cols = np.zeros((2 * LANES, SIDE))
    cols[:HALF] = cos_image
    cols[LANES : LANES + HALF] = sin_image
    tap_rows = np.zeros((SPAN, TAP_ROWS))
    tap_rows[:, :TAPS] = np.concatenate([cos_taps, sin_taps], axis=0)
    tap_cols = np.zeros((TAP_LANES, 2 * LANES))
    tap_cols[:TAPS, :HALF] = cos_taps.T
    tap_cols[:TAPS, LANES : LANES + HALF] = sin_taps.T
    return (
        np.asarray(rows, low),
        np.asarray(rows.T, low),
        np.asarray(cols, low),
        np.asarray(cols.T, low),
        np.asarray(np.concatenate([tap_rows, tap_rows], axis=1), low),
        np.asarray(np.concatenate([tap_cols, tap_cols], axis=0), low),
    )


def dot(left, right):
    return lax.dot_general(
        left, right, (((1,), (0,)), ((), ())), preferred_element_type=jnp.float32
    )


def split_low(values):
    high = values.astype(jnp.bfloat16)
    return high, (values - high.astype(jnp.float32)).astype(jnp.bfloat16)


def strip_loop(order_ref, strip_rows, channels, body):
    strips = S // strip_rows

    def step(index, carry):
        cell = index // strips
        strip = index % strips
        device = order_ref[cell] * strips + strip
        base = (cell // 2) * S + strip * strip_rows
        pixel_base = device * (strip_rows * S)
        for row in range(strip_rows):
            body(
                cell % 2,
                device,
                pl.ds(row * S, S),
                pl.ds(base + row, channels, stride=SIDE),
                pl.ds(pl.multiple_of(pixel_base + row * S, S), S),
            )
        return carry

    lax.fori_loop(0, PATCHES * strips, step, 0)


def channel_rows(channel):
    return pl.ds(pl.multiple_of(channel * SIDE, SIDE), SIDE)


def signed_pair(values):
    cc, cs = values[:HALF, :LANES], values[:HALF, LANES:]
    sc, ss = values[HALF:, :LANES], values[HALF:, LANES:]
    return cc - ss, sc + cs, cc + ss, sc - cs


def prepare_kernel(
    strip_rows, order_ref, data_ref, taps_ref, tap_rows_ref, tap_cols_ref, beam_ref, image_ref, stack_ref
):
    channels = data_ref.shape[0]

    def spread(cell_col, device, lanes, spread_rows, pixels):
        stack_ref[cell_col, spread_rows, :] = data_ref[:, pixels].astype(jnp.float32)

    def channel_step(channel, carry):
        tap_high, tap_low = split_low(taps_ref[channel])
        tap_first = dot(tap_rows_ref[...], jnp.concatenate([tap_high, tap_low], axis=0))
        first_high, first_low = split_low(tap_first * (2.0 / (SPAN * SPAN)))
        spectrum = dot(jnp.concatenate([first_high, first_low], axis=1), tap_cols_ref[...])
        for part, values in enumerate(signed_pair(spectrum)):
            beam_ref[channel, part] = values
        here = channel_rows(channel)
        image_ref[channel, :, :S] = stack_ref[0, here, :].astype(jnp.bfloat16)
        image_ref[channel, :, S:] = stack_ref[1, here, :].astype(jnp.bfloat16)
        return carry

    strip_loop(order_ref, strip_rows, channels, spread)
    lax.fori_loop(0, channels, channel_step, 0)


def prepare(order, data, taps, strip_rows):
    channels, pixels = data.shape
    constants = tables()[4:]
    whole = pl.BlockSpec(memory_space=pltpu.VMEM)
    return pl.pallas_call(
        functools.partial(prepare_kernel, strip_rows),
        out_shape=(
            jax.ShapeDtypeStruct((channels, 4, HALF, LANES), jnp.float32),
            jax.ShapeDtypeStruct((channels, SIDE, SIDE), jnp.bfloat16),
        ),
        grid=(channels // BLOCK,),
        in_specs=[
            pl.BlockSpec(memory_space=pltpu.SMEM),
            pl.BlockSpec((BLOCK, pixels), lambda i: (i, 0)),
            pl.BlockSpec((BLOCK, TAP_ROWS, TAP_LANES), lambda i: (i, 0, 0)),
            whole,
            whole,
        ],
        out_specs=(
            pl.BlockSpec((BLOCK, 4, HALF, LANES), lambda i: (i, 0, 0, 0)),
            pl.BlockSpec((BLOCK, SIDE, SIDE), lambda i: (i, 0, 0)),
        ),
        scratch_shapes=[pltpu.VMEM((2, BLOCK * SIDE, S), jnp.float32)],
        compiler_params=pltpu.CompilerParams(vmem_limit_bytes=VMEM_BYTES),
        cost_estimate=pl.CostEstimate(
            flops=2 * channels * 1440 * 65536, bytes_accessed=28 << 20, transcendentals=0
        ),
    )(order, data, taps, *constants)


def convolve_kernel(
    strip_rows,
    first_channel,
    order_ref,
    noise_ref,
    earlier_ref,
    sky_ref,
    beam_ref,
    data_ref,
    rows_ref,
    rows_t_ref,
    cols_ref,
    cols_t_ref,
    residual_ref,
    grad_ref,
    misfit_ref,
    stack_ref,
):
    channel = pl.program_id(0)
    channels = sky_ref.shape[1]

    def spread(cell_col, device, lanes, spread_rows, pixels):
        stack_ref[cell_col, spread_rows, :] = sky_ref[device, :, lanes].astype(jnp.float32)

    def gather(cell_col, device, lanes, spread_rows, pixels):
        grad_ref[device, :, lanes] = stack_ref[cell_col, spread_rows, :].astype(jnp.bfloat16)

    def filter_image(image, conjugate):
        first = dot(rows_ref[...], image).astype(jnp.bfloat16)
        re_plus, im_plus, re_minus, im_minus = signed_pair(dot(first, cols_t_ref[...]))
        beam_re_plus, beam_im_plus, beam_re_minus, beam_im_minus = (
            beam_ref[0, 0],
            beam_ref[0, 1],
            beam_ref[0, 2],
            beam_ref[0, 3],
        )
        if conjugate:
            out_re_plus = re_plus * beam_re_plus + im_plus * beam_im_plus
            out_im_plus = im_plus * beam_re_plus - re_plus * beam_im_plus
            out_re_minus = re_minus * beam_re_minus + im_minus * beam_im_minus
            out_im_minus = im_minus * beam_re_minus - re_minus * beam_im_minus
        else:
            out_re_plus = re_plus * beam_re_plus - im_plus * beam_im_plus
            out_im_plus = im_plus * beam_re_plus + re_plus * beam_im_plus
            out_re_minus = re_minus * beam_re_minus - im_minus * beam_im_minus
            out_im_minus = im_minus * beam_re_minus + re_minus * beam_im_minus
        product = jnp.concatenate(
            [
                jnp.concatenate([out_re_plus + out_re_minus, out_im_plus - out_im_minus], axis=1),
                jnp.concatenate([out_im_plus + out_im_minus, out_re_minus - out_re_plus], axis=1),
            ],
            axis=0,
        ).astype(jnp.bfloat16)
        second = dot(product, cols_ref[...]).astype(jnp.bfloat16)
        return dot(rows_t_ref[...], second)

    @pl.when(channel == 0)
    def _():
        misfit_ref[...] = earlier_ref[...]
        strip_loop(order_ref, strip_rows, channels, spread)

    here = channel_rows(channel)
    image = jnp.concatenate([stack_ref[0, here, :], stack_ref[1, here, :]], axis=1)
    residual = filter_image(image.astype(jnp.bfloat16), True) - data_ref[0].astype(jnp.float32)
    residual_ref[0] = residual.astype(jnp.bfloat16)
    weighted = noise_ref[first_channel + channel] * residual
    misfit_ref[...] += jnp.sum((weighted * residual).reshape(SIDE // 8, 8, SIDE), axis=0)
    grad = filter_image(weighted.astype(jnp.bfloat16), False) * image
    stack_ref[0, here, :] = grad[:, :S]
    stack_ref[1, here, :] = grad[:, S:]

    @pl.when(channel == channels - 1)
    def _():
        strip_loop(order_ref, strip_rows, channels, gather)
        strip = strip_rows * S
        if grad_ref.shape[2] > strip:
            total = jnp.full((channels, S), jnp.sum(misfit_ref[...]), jnp.float32)
            high, rest = split_low(total)
            middle = rest.astype(jnp.float32)
            low = total - high.astype(jnp.float32) - middle
            lane = lax.broadcasted_iota(jnp.int32, (channels, S), 1)
            terms = jnp.where(lane == 0, high.astype(jnp.float32), jnp.where(lane == 1, middle, low))
            terms = jnp.where(lane < 3, terms, 0.0).astype(jnp.bfloat16)
            for device in range(grad_ref.shape[0]):
                grad_ref[device, :, strip:] = terms


def convolve(order, noise_weight, earlier, sky, beam, data_images, chunk, extra):
    devices, channels, strip = sky.shape
    smem = pl.BlockSpec(memory_space=pltpu.SMEM)
    whole = pl.BlockSpec(memory_space=pltpu.VMEM)
    constants = tables()[:4]
    first_channel = chunk * channels
    return pl.pallas_call(
        functools.partial(convolve_kernel, strip // S, first_channel),
        out_shape=(
            jax.ShapeDtypeStruct((channels, SIDE, SIDE), jnp.bfloat16),
            jax.ShapeDtypeStruct((devices, channels, strip + extra), jnp.bfloat16),
            jax.ShapeDtypeStruct((8, SIDE), jnp.float32),
        ),
        grid=(channels,),
        in_specs=[
            smem,
            smem,
            whole,
            whole,
            pl.BlockSpec((1, 4, HALF, LANES), lambda i: (first_channel + i, 0, 0, 0)),
            pl.BlockSpec((1, SIDE, SIDE), lambda i: (first_channel + i, 0, 0)),
        ]
        + [whole] * len(constants),
        out_specs=(pl.BlockSpec((1, SIDE, SIDE), lambda i: (i, 0, 0)), whole, whole),
        scratch_shapes=[pltpu.VMEM((2, channels * SIDE, S), jnp.float32)],
        compiler_params=pltpu.CompilerParams(vmem_limit_bytes=VMEM_BYTES),
        cost_estimate=pl.CostEstimate(
            flops=2 * channels * 2 * 1952 * 65536, bytes_accessed=24 << 20, transcendentals=0
        ),
    )(order, noise_weight, earlier, sky, beam, data_images, *constants)


def flatten_kernel(strip_rows, order_ref, *refs):
    image_refs, flat_ref, stack_ref = refs[:-2], refs[-2], refs[-1]
    for chunk, image_ref in enumerate(image_refs):
        channels = image_ref.shape[0]
        rows = slice(chunk * channels, (chunk + 1) * channels)

        def channel_step(channel, carry):
            here = channel_rows(channel)
            image = image_ref[channel].astype(jnp.float32)
            stack_ref[0, here, :] = image[:, :S]
            stack_ref[1, here, :] = image[:, S:]
            return carry

        def gather(cell_col, device, lanes, spread_rows, pixels):
            flat_ref[rows, pixels] = stack_ref[cell_col, spread_rows, :].astype(jnp.bfloat16)

        lax.fori_loop(0, channels, channel_step, 0)
        strip_loop(order_ref, strip_rows, channels, gather)


def flatten(order, images, strip_rows):
    channels = sum(part.shape[0] for part in images)
    whole = pl.BlockSpec(memory_space=pltpu.VMEM)
    return pl.pallas_call(
        functools.partial(flatten_kernel, strip_rows),
        out_shape=jax.ShapeDtypeStruct((channels, SIDE * SIDE), jnp.bfloat16),
        in_specs=[pl.BlockSpec(memory_space=pltpu.SMEM)] + [whole] * len(images),
        out_specs=whole,
        scratch_shapes=[pltpu.VMEM((2, images[0].shape[0] * SIDE, S), jnp.float32)],
        compiler_params=pltpu.CompilerParams(vmem_limit_bytes=FLATTEN_VMEM_BYTES),
        cost_estimate=pl.CostEstimate(flops=1 << 20, bytes_accessed=32 << 20, transcendentals=0),
    )(order, *images)


def sky_kernel(chunk, root_ref, level_ref, latent_ref, sky_ref):
    devices, _, channels, freqs = root_ref.shape
    pixels = latent_ref.shape[0]
    root = root_ref[:, 0].reshape(devices * channels, freqs)
    log_sky = lax.dot_general(
        root,
        latent_ref[...].astype(jnp.bfloat16),
        (((1,), (1,)), ((), ())),
        preferred_element_type=jnp.float32,
    )
    level = jnp.broadcast_to(level_ref[...], (S, freqs)).T.reshape(devices, -1, channels, S)
    level = level[:, chunk].reshape(devices * channels, S)
    for first in range(0, pixels, S):
        sky = jnp.exp(log_sky[:, first : first + S] + level).astype(jnp.bfloat16)
        sky_ref[:, :, first : first + S] = sky.reshape(devices, channels, S)


def brightness(chunk, root_parts, log_level, latent):
    devices, _, channels, freqs = root_parts.shape
    pixels = latent.shape[0]
    return pl.pallas_call(
        functools.partial(sky_kernel, chunk),
        out_shape=jax.ShapeDtypeStruct((devices, channels, pixels), jnp.bfloat16),
        grid=(pixels // SKY_BLOCK,),
        in_specs=[
            pl.BlockSpec((devices, 1, channels, freqs), lambda i: (0, chunk, 0, 0)),
            pl.BlockSpec((1, freqs), lambda i: (0, 0)),
            pl.BlockSpec((SKY_BLOCK, freqs), lambda i: (i, 0)),
        ],
        out_specs=pl.BlockSpec((devices, channels, SKY_BLOCK), lambda i: (0, 0, i)),
        compiler_params=pltpu.CompilerParams(vmem_limit_bytes=VMEM_BYTES),
        cost_estimate=pl.CostEstimate(
            flops=2 * pixels * freqs * devices * channels,
            bytes_accessed=10 << 20,
            transcendentals=pixels * devices * channels,
        ),
    )(root_parts, log_level.reshape(1, freqs), latent)


def pull_back(chunk, grad_ref, root_ref, here):
    devices, channels, _ = grad_ref.shape
    return lax.dot_general(
        grad_ref[:, :, here].reshape(devices * channels, here.size),
        root_ref[:, chunk].reshape(devices * channels, -1),
        (((0,), (0,)), ((), ())),
        preferred_element_type=jnp.float32,
    )


def kick_kernel(momentum_ref, latent_ref, root_ref, *refs):
    grad_refs, kicked_ref = refs[:-1], refs[-1]
    pixels = latent_ref.shape[0]
    here = pl.ds(pl.multiple_of(pl.program_id(0) * pixels, pixels), pixels)

    force = latent_ref[...]
    for chunk, grad_ref in enumerate(grad_refs):
        force = force + pull_back(chunk, grad_ref, root_ref, here)
    kicked_ref[...] = momentum_ref[...] - leap_size * force


def kick(momentum, latent, root_parts, grads):
    pixels, freqs = latent.shape
    block = pl.BlockSpec((PIXEL_BLOCK, freqs), lambda i: (i, 0))
    whole = pl.BlockSpec(memory_space=pltpu.VMEM)
    return pl.pallas_call(
        kick_kernel,
        out_shape=jax.ShapeDtypeStruct(latent.shape, jnp.float32),
        grid=(pixels // PIXEL_BLOCK,),
        in_specs=[block, block] + [whole] * (1 + len(grads)),
        out_specs=block,
        compiler_params=pltpu.CompilerParams(vmem_limit_bytes=FLATTEN_VMEM_BYTES),
        cost_estimate=pl.CostEstimate(
            flops=2 * pixels * freqs * 256, bytes_accessed=26 << 20, transcendentals=0
        ),
    )(momentum, latent, root_parts, *grads)


def leap_kernel(
    chunk,
    scale,
    kicked_ref,
    latent_ref,
    grad_ref,
    terms_ref,
    root_ref,
    latent_out_ref,
    momentum_out_ref,
    misfit_ref,
):
    pixels = momentum_out_ref.shape[0]
    grad_latent = pull_back(chunk, grad_ref, root_ref, pl.ds(0, pixels))
    momentum = kicked_ref[...] - leap_size * grad_latent
    momentum_out_ref[...] = momentum
    latent_out_ref[...] = latent_ref[...] + leap_size * momentum

    @pl.when(pl.program_id(0) == 0)
    def _():
        terms = terms_ref[...].astype(jnp.float32)
        row = lax.broadcasted_iota(jnp.int32, terms.shape, 1)
        misfit_ref[0] = scale * jnp.sum(jnp.where(row == 0, terms, 0.0))


def leap(chunk, scale, kicked, latent, grad, root_parts):
    pixels, freqs = latent.shape
    whole = pl.BlockSpec(memory_space=pltpu.VMEM)
    far_grad = pltpu.with_memory_space_constraint(grad, pltpu.HBM)
    block = pl.BlockSpec((PIXEL_BLOCK, freqs), lambda i: (i, 0))
    return pl.pallas_call(
        functools.partial(leap_kernel, chunk, scale),
        out_shape=(jax.ShapeDtypeStruct(latent.shape, jnp.float32),) * 2
        + (jax.ShapeDtypeStruct((1,), jnp.float32),),
        grid=(pixels // PIXEL_BLOCK,),
        in_specs=[block, block, pl.BlockSpec(grad.shape[:2] + (PIXEL_BLOCK,), lambda i: (0, 0, i)), pl.BlockSpec(grad.shape[:2] + (S,), lambda i: (0, 0, pixels // S)), whole],
        out_specs=(block, block, pl.BlockSpec(memory_space=pltpu.SMEM)),
        compiler_params=pltpu.CompilerParams(vmem_limit_bytes=VMEM_BYTES),
        cost_estimate=pl.CostEstimate(
            flops=2 * pixels * freqs * 256, bytes_accessed=34 << 20, transcendentals=0
        ),
    )(kicked, latent, far_grad, far_grad, root_parts)


def cell_order(neighbours):
    has_above = neighbours[:, 1] != -1
    has_left = neighbours[:, 3] != -1
    cells = 2 * has_above.astype(jnp.int32) + has_left.astype(jnp.int32)
    patch_ids = jnp.arange(PATCHES, dtype=jnp.int32)
    match = cells[None, :] == patch_ids[:, None]
    return jnp.sum(jnp.where(match, patch_ids[None, :], 0), axis=1)


def masked_taps(beam_taps, beam_radius):
    offsets = jnp.arange(TAPS, dtype=jnp.int32) - R
    distance = offsets[:, None] * offsets[:, None] + offsets[None, :] * offsets[None, :]
    inside = distance[None, :, :] <= (beam_radius * beam_radius)[:, None, None]
    kernel = jnp.where(inside, beam_taps, jnp.zeros_like(beam_taps))
    return jnp.pad(kernel, ((0, 0), (0, TAP_ROWS - TAPS), (0, TAP_LANES - TAPS)))


def shards(
    latent,
    momentum,
    data,
    neighbours,
    spectral_root,
    log_level,
    beam_taps,
    beam_radius,
    noise_weight,
):
    devices = lax.axis_size("pix")
    pix_dev = latent.shape[0]
    chan_dev = data.shape[0]
    freqs = spectral_root.shape[0]
    chunks = chan_dev // BLOCK
    root_parts = spectral_root.reshape(devices, chunks, BLOCK, freqs)
    order = cell_order(neighbours)
    taps = masked_taps(beam_taps, beam_radius)

    strip_rows = pix_dev // S
    beam, data_images = prepare(order, data, taps, strip_rows)

    skies = []
    for chunk in range(chunks):
        level = log_level
        if chunk == 1:
            level, beam, data_images = lax.optimization_barrier((level, beam, data_images))
        skies.append(brightness(chunk, root_parts, level, latent))

    residuals, grads = [], []
    partial = jnp.zeros((8, SIDE), jnp.float32)
    for chunk in range(chunks):
        extra = S if chunk == chunks - 1 else 0
        sky = lax.all_to_all(skies[chunk], "pix", split_axis=0, concat_axis=0, tiled=True)
        residual, grad, partial = convolve(
            order, noise_weight, partial, sky, beam, data_images, chunk, extra
        )
        residuals.append(residual)
        grads.append(lax.all_to_all(grad, "pix", split_axis=0, concat_axis=0, tiled=True))

    residual_maps = flatten(order, residuals, strip_rows)
    kicked = kick(momentum, latent, root_parts, grads[:-1])
    scale = 0.5 / (freqs * devices * pix_dev)
    new_latent, new_momentum, misfit = leap(
        chunks - 1, scale, kicked, latent, grads[-1], root_parts
    )
    return (new_latent, new_momentum, residual_maps, misfit)


def solution(mesh):
    placed = (
        P(("chain", "pix"), None),
        P(("chain", "pix"), None),
        P("pix", "chain"),
        P("chain", None),
        P(),
        P(),
        P("pix", None, None),
        P("pix"),
        P("pix"),
    )
    return jax.shard_map(
        shards,
        mesh=mesh,
        in_specs=placed,
        out_specs=(
            P(("chain", "pix"), None),
            P(("chain", "pix"), None),
            P("pix", "chain"),
            P("chain"),
        ),
        check_vma=False,
    )
```

```python
import functools
import math

import jax
import jax.numpy as jnp
import numpy as np
from jax import lax
from jax.experimental import pallas as pl
from jax.experimental.pallas import tpu as pltpu
from jax.sharding import PartitionSpec as P

S = 128
R = 32
PATCHES = 4
TAPS = 65
SIDE = 2 * S
SPAN = SIDE + R
HALF = SPAN // 2
LANES = 256
TAP_ROWS = 80
TAP_LANES = 128
BLOCK = 16
VMEM_BYTES = 56 * 1024 * 1024
FLATTEN_VMEM_BYTES = 24 * 1024 * 1024
PIXEL_BLOCK = 1024
LEAP_BLOCK = 2048
SKY_BLOCK = 2048

leap_size = 0.25


def half_tables(positions):
    angle = 2.0 * math.pi / SPAN * (np.arange(HALF)[:, None] + 0.5) * positions[None, :]
    return np.cos(angle), np.sin(angle)


def tables():
    low = jnp.bfloat16
    cos_image, sin_image = half_tables(np.arange(SIDE))
    cos_taps, sin_taps = half_tables(np.arange(TAPS) - R)
    rows = np.concatenate([cos_image, sin_image], axis=0)
    cols = np.zeros((2 * LANES, SIDE))
    cols[:HALF] = cos_image
    cols[LANES : LANES + HALF] = sin_image
    tap_rows = np.zeros((SPAN, TAP_ROWS))
    tap_rows[:, :TAPS] = np.concatenate([cos_taps, sin_taps], axis=0)
    tap_cols = np.zeros((TAP_LANES, 2 * LANES))
    tap_cols[:TAPS, :HALF] = cos_taps.T
    tap_cols[:TAPS, LANES : LANES + HALF] = sin_taps.T
    return (
        np.asarray(rows, low),
        np.asarray(rows.T, low),
        np.asarray(cols, low),
        np.asarray(cols.T, low),
        np.asarray(np.concatenate([tap_rows, tap_rows], axis=1), low),
        np.asarray(np.concatenate([tap_cols, tap_cols], axis=0), low),
    )


def dot(left, right):
    return lax.dot_general(
        left, right, (((1,), (0,)), ((), ())), preferred_element_type=jnp.float32
    )


def split_low(values):
    high = values.astype(jnp.bfloat16)
    return high, (values - high.astype(jnp.float32)).astype(jnp.bfloat16)


def strip_loop(order_ref, strip_rows, channels, body):
    strips = S // strip_rows

    def step(index, carry):
        cell = index // strips
        strip = index % strips
        device = order_ref[cell] * strips + strip
        base = (cell // 2) * S + strip * strip_rows
        pixel_base = device * (strip_rows * S)
        for row in range(strip_rows):
            body(
                cell % 2,
                device,
                pl.ds(row * S, S),
                pl.ds(base + row, channels, stride=SIDE),
                pl.ds(pl.multiple_of(pixel_base + row * S, S), S),
            )
        return carry

    lax.fori_loop(0, PATCHES * strips, step, 0)


def channel_rows(channel):
    return pl.ds(pl.multiple_of(channel * SIDE, SIDE), SIDE)


def signed_pair(values):
    cc, cs = values[:HALF, :LANES], values[:HALF, LANES:]
    sc, ss = values[HALF:, :LANES], values[HALF:, LANES:]
    return cc - ss, sc + cs, cc + ss, sc - cs


def prepare_kernel(
    strip_rows, order_ref, data_ref, taps_ref, tap_rows_ref, tap_cols_ref, beam_ref, image_ref, stack_ref
):
    channels = data_ref.shape[0]

    def spread(cell_col, device, lanes, spread_rows, pixels):
        stack_ref[cell_col, spread_rows, :] = data_ref[:, pixels].astype(jnp.float32)

    def channel_step(channel, carry):
        tap_high, tap_low = split_low(taps_ref[channel])
        tap_first = dot(tap_rows_ref[...], jnp.concatenate([tap_high, tap_low], axis=0))
        first_high, first_low = split_low(tap_first * (2.0 / (SPAN * SPAN)))
        spectrum = dot(jnp.concatenate([first_high, first_low], axis=1), tap_cols_ref[...])
        for part, values in enumerate(signed_pair(spectrum)):
            beam_ref[channel, part] = values
        here = channel_rows(channel)
        image_ref[channel, :, :S] = stack_ref[0, here, :].astype(jnp.bfloat16)
        image_ref[channel, :, S:] = stack_ref[1, here, :].astype(jnp.bfloat16)
        return carry

    strip_loop(order_ref, strip_rows, channels, spread)
    lax.fori_loop(0, channels, channel_step, 0)


def prepare(order, data, taps, strip_rows):
    channels, pixels = data.shape
    constants = tables()[4:]
    whole = pl.BlockSpec(memory_space=pltpu.VMEM)
    return pl.pallas_call(
        functools.partial(prepare_kernel, strip_rows),
        out_shape=(
            jax.ShapeDtypeStruct((channels, 4, HALF, LANES), jnp.float32),
            jax.ShapeDtypeStruct((channels, SIDE, SIDE), jnp.bfloat16),
        ),
        grid=(channels // BLOCK,),
        in_specs=[
            pl.BlockSpec(memory_space=pltpu.SMEM),
            pl.BlockSpec((BLOCK, pixels), lambda i: (i, 0)),
            pl.BlockSpec((BLOCK, TAP_ROWS, TAP_LANES), lambda i: (i, 0, 0)),
            whole,
            whole,
        ],
        out_specs=(
            pl.BlockSpec((BLOCK, 4, HALF, LANES), lambda i: (i, 0, 0, 0)),
            pl.BlockSpec((BLOCK, SIDE, SIDE), lambda i: (i, 0, 0)),
        ),
        scratch_shapes=[pltpu.VMEM((2, BLOCK * SIDE, S), jnp.float32)],
        compiler_params=pltpu.CompilerParams(vmem_limit_bytes=VMEM_BYTES),
        cost_estimate=pl.CostEstimate(
            flops=2 * channels * 1440 * 65536, bytes_accessed=28 << 20, transcendentals=0
        ),
    )(order, data, taps, *constants)


def convolve_kernel(
    strip_rows,
    first_channel,
    order_ref,
    noise_ref,
    earlier_ref,
    sky_ref,
    beam_ref,
    data_ref,
    rows_ref,
    rows_t_ref,
    cols_ref,
    cols_t_ref,
    residual_ref,
    grad_ref,
    misfit_ref,
    stack_ref,
):
    channel = pl.program_id(0)
    channels = sky_ref.shape[1]

    def spread(cell_col, device, lanes, spread_rows, pixels):
        stack_ref[cell_col, spread_rows, :] = sky_ref[device, :, lanes].astype(jnp.float32)

    def gather(cell_col, device, lanes, spread_rows, pixels):
        grad_ref[device, :, lanes] = stack_ref[cell_col, spread_rows, :].astype(jnp.bfloat16)

    def filter_image(image, conjugate):
        first = dot(rows_ref[...], image).astype(jnp.bfloat16)
        re_plus, im_plus, re_minus, im_minus = signed_pair(dot(first, cols_t_ref[...]))
        beam_re_plus, beam_im_plus, beam_re_minus, beam_im_minus = (
            beam_ref[0, 0],
            beam_ref[0, 1],
            beam_ref[0, 2],
            beam_ref[0, 3],
        )
        if conjugate:
            out_re_plus = re_plus * beam_re_plus + im_plus * beam_im_plus
            out_im_plus = im_plus * beam_re_plus - re_plus * beam_im_plus
            out_re_minus = re_minus * beam_re_minus + im_minus * beam_im_minus
            out_im_minus = im_minus * beam_re_minus - re_minus * beam_im_minus
        else:
            out_re_plus = re_plus * beam_re_plus - im_plus * beam_im_plus
            out_im_plus = im_plus * beam_re_plus + re_plus * beam_im_plus
            out_re_minus = re_minus * beam_re_minus - im_minus * beam_im_minus
            out_im_minus = im_minus * beam_re_minus + re_minus * beam_im_minus
        product = jnp.concatenate(
            [
                jnp.concatenate([out_re_plus + out_re_minus, out_im_plus - out_im_minus], axis=1),
                jnp.concatenate([out_im_plus + out_im_minus, out_re_minus - out_re_plus], axis=1),
            ],
            axis=0,
        ).astype(jnp.bfloat16)
        second = dot(product, cols_ref[...]).astype(jnp.bfloat16)
        return dot(rows_t_ref[...], second)

    @pl.when(channel == 0)
    def _():
        misfit_ref[...] = earlier_ref[...]
        strip_loop(order_ref, strip_rows, channels, spread)

    here = channel_rows(channel)
    image = jnp.concatenate([stack_ref[0, here, :], stack_ref[1, here, :]], axis=1)
    residual = filter_image(image.astype(jnp.bfloat16), True) - data_ref[0].astype(jnp.float32)
    residual_ref[0] = residual.astype(jnp.bfloat16)
    weighted = noise_ref[first_channel + channel] * residual
    misfit_ref[...] += jnp.sum((weighted * residual).reshape(SIDE // 8, 8, SIDE), axis=0)
    grad = filter_image(weighted.astype(jnp.bfloat16), False) * image
    stack_ref[0, here, :] = grad[:, :S]
    stack_ref[1, here, :] = grad[:, S:]

    @pl.when(channel == channels - 1)
    def _():
        strip_loop(order_ref, strip_rows, channels, gather)
        strip = strip_rows * S
        if grad_ref.shape[2] > strip:
            total = jnp.full((channels, S), jnp.sum(misfit_ref[...]), jnp.float32)
            high, rest = split_low(total)
            middle = rest.astype(jnp.float32)
            low = total - high.astype(jnp.float32) - middle
            lane = lax.broadcasted_iota(jnp.int32, (channels, S), 1)
            terms = jnp.where(lane == 0, high.astype(jnp.float32), jnp.where(lane == 1, middle, low))
            terms = jnp.where(lane < 3, terms, 0.0).astype(jnp.bfloat16)
            for device in range(grad_ref.shape[0]):
                grad_ref[device, :, strip:] = terms


def convolve(order, noise_weight, earlier, sky, beam, data_images, chunk, extra):
    devices, channels, strip = sky.shape
    smem = pl.BlockSpec(memory_space=pltpu.SMEM)
    whole = pl.BlockSpec(memory_space=pltpu.VMEM)
    constants = tables()[:4]
    first_channel = chunk * channels
    return pl.pallas_call(
        functools.partial(convolve_kernel, strip // S, first_channel),
        out_shape=(
            jax.ShapeDtypeStruct((channels, SIDE, SIDE), jnp.bfloat16),
            jax.ShapeDtypeStruct((devices, channels, strip + extra), jnp.bfloat16),
            jax.ShapeDtypeStruct((8, SIDE), jnp.float32),
        ),
        grid=(channels,),
        in_specs=[
            smem,
            smem,
            whole,
            whole,
            pl.BlockSpec((1, 4, HALF, LANES), lambda i: (first_channel + i, 0, 0, 0)),
            pl.BlockSpec((1, SIDE, SIDE), lambda i: (first_channel + i, 0, 0)),
        ]
        + [whole] * len(constants),
        out_specs=(pl.BlockSpec((1, SIDE, SIDE), lambda i: (i, 0, 0)), whole, whole),
        scratch_shapes=[pltpu.VMEM((2, channels * SIDE, S), jnp.float32)],
        compiler_params=pltpu.CompilerParams(vmem_limit_bytes=VMEM_BYTES),
        cost_estimate=pl.CostEstimate(
            flops=2 * channels * 2 * 1952 * 65536, bytes_accessed=24 << 20, transcendentals=0
        ),
    )(order, noise_weight, earlier, sky, beam, data_images, *constants)


def flatten_kernel(strip_rows, order_ref, *refs):
    image_refs, flat_ref, stack_ref = refs[:-2], refs[-2], refs[-1]
    for chunk, image_ref in enumerate(image_refs):
        channels = image_ref.shape[0]
        rows = slice(chunk * channels, (chunk + 1) * channels)

        def channel_step(channel, carry):
            here = channel_rows(channel)
            image = image_ref[channel].astype(jnp.float32)
            stack_ref[0, here, :] = image[:, :S]
            stack_ref[1, here, :] = image[:, S:]
            return carry

        def gather(cell_col, device, lanes, spread_rows, pixels):
            flat_ref[rows, pixels] = stack_ref[cell_col, spread_rows, :].astype(jnp.bfloat16)

        lax.fori_loop(0, channels, channel_step, 0)
        strip_loop(order_ref, strip_rows, channels, gather)


def flatten(order, images, strip_rows):
    channels = sum(part.shape[0] for part in images)
    whole = pl.BlockSpec(memory_space=pltpu.VMEM)
    return pl.pallas_call(
        functools.partial(flatten_kernel, strip_rows),
        out_shape=jax.ShapeDtypeStruct((channels, SIDE * SIDE), jnp.bfloat16),
        in_specs=[pl.BlockSpec(memory_space=pltpu.SMEM)] + [whole] * len(images),
        out_specs=whole,
        scratch_shapes=[pltpu.VMEM((2, images[0].shape[0] * SIDE, S), jnp.float32)],
        compiler_params=pltpu.CompilerParams(vmem_limit_bytes=FLATTEN_VMEM_BYTES),
        cost_estimate=pl.CostEstimate(flops=1 << 20, bytes_accessed=32 << 20, transcendentals=0),
    )(order, *images)


def sky_kernel(chunk, root_ref, level_ref, latent_ref, sky_ref):
    devices, _, channels, freqs = root_ref.shape
    pixels = latent_ref.shape[0]
    root = root_ref[:, 0].reshape(devices * channels, freqs)
    log_sky = lax.dot_general(
        root,
        latent_ref[...].astype(jnp.bfloat16),
        (((1,), (1,)), ((), ())),
        preferred_element_type=jnp.float32,
    )
    level = jnp.broadcast_to(level_ref[...], (S, freqs)).T.reshape(devices, -1, channels, S)
    level = level[:, chunk].reshape(devices * channels, S)
    for first in range(0, pixels, S):
        sky = jnp.exp(log_sky[:, first : first + S] + level).astype(jnp.bfloat16)
        sky_ref[:, :, first : first + S] = sky.reshape(devices, channels, S)


def brightness(chunk, root_parts, log_level, latent):
    devices, _, channels, freqs = root_parts.shape
    pixels = latent.shape[0]
    return pl.pallas_call(
        functools.partial(sky_kernel, chunk),
        out_shape=jax.ShapeDtypeStruct((devices, channels, pixels), jnp.bfloat16),
        grid=(pixels // SKY_BLOCK,),
        in_specs=[
            pl.BlockSpec((devices, 1, channels, freqs), lambda i: (0, chunk, 0, 0)),
            pl.BlockSpec((1, freqs), lambda i: (0, 0)),
            pl.BlockSpec((SKY_BLOCK, freqs), lambda i: (i, 0)),
        ],
        out_specs=pl.BlockSpec((devices, channels, SKY_BLOCK), lambda i: (0, 0, i)),
        compiler_params=pltpu.CompilerParams(vmem_limit_bytes=VMEM_BYTES),
        cost_estimate=pl.CostEstimate(
            flops=2 * pixels * freqs * devices * channels,
            bytes_accessed=10 << 20,
            transcendentals=pixels * devices * channels,
        ),
    )(root_parts, log_level.reshape(1, freqs), latent)


def pull_back(chunk, grad_ref, root_ref, here):
    devices, channels, _ = grad_ref.shape
    return lax.dot_general(
        grad_ref[:, :, here].reshape(devices * channels, here.size),
        root_ref[:, chunk].reshape(devices * channels, -1),
        (((0,), (0,)), ((), ())),
        preferred_element_type=jnp.float32,
    )


def kick_kernel(momentum_ref, latent_ref, root_ref, *refs):
    grad_refs, kicked_ref = refs[:-1], refs[-1]
    pixels = latent_ref.shape[0]
    here = pl.ds(pl.multiple_of(pl.program_id(0) * pixels, pixels), pixels)

    force = latent_ref[...]
    for chunk, grad_ref in enumerate(grad_refs):
        force = force + pull_back(chunk, grad_ref, root_ref, here)
    kicked_ref[...] = momentum_ref[...] - leap_size * force


def kick(momentum, latent, root_parts, grads):
    pixels, freqs = latent.shape
    block = pl.BlockSpec((PIXEL_BLOCK, freqs), lambda i: (i, 0))
    whole = pl.BlockSpec(memory_space=pltpu.VMEM)
    return pl.pallas_call(
        kick_kernel,
        out_shape=jax.ShapeDtypeStruct(latent.shape, jnp.float32),
        grid=(pixels // PIXEL_BLOCK,),
        in_specs=[block, block] + [whole] * (1 + len(grads)),
        out_specs=block,
        compiler_params=pltpu.CompilerParams(vmem_limit_bytes=FLATTEN_VMEM_BYTES),
        cost_estimate=pl.CostEstimate(
            flops=2 * pixels * freqs * 256, bytes_accessed=26 << 20, transcendentals=0
        ),
    )(momentum, latent, root_parts, *grads)


def leap_kernel(
    chunk,
    scale,
    kicked_ref,
    latent_ref,
    grad_ref,
    terms_ref,
    root_ref,
    latent_out_ref,
    momentum_out_ref,
    misfit_ref,
):
    pixels = momentum_out_ref.shape[0]
    grad_latent = pull_back(chunk, grad_ref, root_ref, pl.ds(0, pixels))
    momentum = kicked_ref[...] - leap_size * grad_latent
    momentum_out_ref[...] = momentum
    latent_out_ref[...] = latent_ref[...] + leap_size * momentum

    @pl.when(pl.program_id(0) == 0)
    def _():
        terms = terms_ref[...].astype(jnp.float32)
        row = lax.broadcasted_iota(jnp.int32, terms.shape, 1)
        misfit_ref[0] = scale * jnp.sum(jnp.where(row == 0, terms, 0.0))


def leap(chunk, scale, kicked, latent, grad, root_parts):
    pixels, freqs = latent.shape
    whole = pl.BlockSpec(memory_space=pltpu.VMEM)
    far_grad = pltpu.with_memory_space_constraint(grad, pltpu.HBM)
    block = pl.BlockSpec((LEAP_BLOCK, freqs), lambda i: (i, 0))
    return pl.pallas_call(
        functools.partial(leap_kernel, chunk, scale),
        out_shape=(jax.ShapeDtypeStruct(latent.shape, jnp.float32),) * 2
        + (jax.ShapeDtypeStruct((1,), jnp.float32),),
        grid=(pixels // LEAP_BLOCK,),
        in_specs=[block, block, pl.BlockSpec(grad.shape[:2] + (LEAP_BLOCK,), lambda i: (0, 0, i)), pl.BlockSpec(grad.shape[:2] + (S,), lambda i: (0, 0, pixels // S)), whole],
        out_specs=(block, block, pl.BlockSpec(memory_space=pltpu.SMEM)),
        compiler_params=pltpu.CompilerParams(vmem_limit_bytes=VMEM_BYTES),
        cost_estimate=pl.CostEstimate(
            flops=2 * pixels * freqs * 256, bytes_accessed=34 << 20, transcendentals=0
        ),
    )(kicked, latent, far_grad, far_grad, root_parts)


def cell_order(neighbours):
    has_above = neighbours[:, 1] != -1
    has_left = neighbours[:, 3] != -1
    cells = 2 * has_above.astype(jnp.int32) + has_left.astype(jnp.int32)
    patch_ids = jnp.arange(PATCHES, dtype=jnp.int32)
    match = cells[None, :] == patch_ids[:, None]
    return jnp.sum(jnp.where(match, patch_ids[None, :], 0), axis=1)


def masked_taps(beam_taps, beam_radius):
    offsets = jnp.arange(TAPS, dtype=jnp.int32) - R
    distance = offsets[:, None] * offsets[:, None] + offsets[None, :] * offsets[None, :]
    inside = distance[None, :, :] <= (beam_radius * beam_radius)[:, None, None]
    kernel = jnp.where(inside, beam_taps, jnp.zeros_like(beam_taps))
    return jnp.pad(kernel, ((0, 0), (0, TAP_ROWS - TAPS), (0, TAP_LANES - TAPS)))


def shards(
    latent,
    momentum,
    data,
    neighbours,
    spectral_root,
    log_level,
    beam_taps,
    beam_radius,
    noise_weight,
):
    devices = lax.axis_size("pix")
    pix_dev = latent.shape[0]
    chan_dev = data.shape[0]
    freqs = spectral_root.shape[0]
    chunks = chan_dev // BLOCK
    root_parts = spectral_root.reshape(devices, chunks, BLOCK, freqs)
    order = cell_order(neighbours)
    taps = masked_taps(beam_taps, beam_radius)

    strip_rows = pix_dev // S
    beam, data_images = prepare(order, data, taps, strip_rows)

    skies = []
    for chunk in range(chunks):
        level = log_level
        if chunk == 1:
            level, beam, data_images = lax.optimization_barrier((level, beam, data_images))
        skies.append(brightness(chunk, root_parts, level, latent))

    residuals, grads = [], []
    partial = jnp.zeros((8, SIDE), jnp.float32)
    for chunk in range(chunks):
        extra = S if chunk == chunks - 1 else 0
        sky = lax.all_to_all(skies[chunk], "pix", split_axis=0, concat_axis=0, tiled=True)
        residual, grad, partial = convolve(
            order, noise_weight, partial, sky, beam, data_images, chunk, extra
        )
        residuals.append(residual)
        grads.append(lax.all_to_all(grad, "pix", split_axis=0, concat_axis=0, tiled=True))

    residual_maps = flatten(order, residuals, strip_rows)
    kicked = kick(momentum, latent, root_parts, grads[:-1])
    scale = 0.5 / (freqs * devices * pix_dev)
    new_latent, new_momentum, misfit = leap(
        chunks - 1, scale, kicked, latent, grads[-1], root_parts
    )
    return (new_latent, new_momentum, residual_maps, misfit)


def solution(mesh):
    placed = (
        P(("chain", "pix"), None),
        P(("chain", "pix"), None),
        P("pix", "chain"),
        P("chain", None),
        P(),
        P(),
        P("pix", None, None),
        P("pix"),
        P("pix"),
    )
    return jax.shard_map(
        shards,
        mesh=mesh,
        in_specs=placed,
        out_specs=(
            P(("chain", "pix"), None),
            P(("chain", "pix"), None),
            P("pix", "chain"),
            P("chain"),
        ),
        check_vma=False,
    )
```
